256 devices in a mesh: pitch: 64 (over x_lo, z, y), span: 4 (over x_hi, core).
Axes of the slice: x: 4 (x_hi: 2, x_lo: 2; x = x_hi * 2 + x_lo), y: 4, z: 8, core: 2. Of those that a mesh axis runs over, the one named last changes fastest.
Arguments:
- stator_adj: float32 [5, 64, 256, 512], P(None, 'pitch', None, 'span'), may hold values from -6 to 6
- rotor_adj: float32 [5, 64, 256, 512], P(None, 'pitch', None, 'span'), may hold values from -6 to 6
- stator_rhs: float32 [5, 64, 256, 512], P(None, 'pitch', None, 'span'), may hold values from -6 to 6
- rotor_rhs: float32 [5, 64, 256, 512], P(None, 'pitch', None, 'span'), may hold values from -6 to 6
- stator_dtau: float32 [64, 256, 512], P('pitch', None, 'span'), may hold values from 0.05 to 0.5
- rotor_dtau: float32 [64, 256, 512], P('pitch', None, 'span'), may hold values from 0.05 to 0.5
- roe_jac: bfloat16 [5, 5, 64, 256, 512], P(None, None, 'pitch', None, 'span'), may hold values from -2.5 to 2.5
- pair_index: int32 [2, 64, 256], P(None, 'pitch'), may hold values from 0 to 511
- pair_weight: float32 [2, 64, 256], P(None, 'pitch'), may hold values from 0.1 to 1
- rot_steps: int32 [2], replicated, may hold values from 0 to 63
Outputs:
- stator_out: float32 [5, 64, 256, 512], P(None, 'pitch', None, 'span')
- rotor_out: float32 [5, 64, 256, 512], P(None, 'pitch', None, 'span')
The draws below stay inside these ranges and needn't reach their ends.
All inputs are finite; a program needn't handle non-finite values.
Results may differ from the reference program's by a relative error of at most 0.0003.
Values sent between devices are 32-bit elements; how exact they have to be, the bound alone decides.
A program may use at most 128 MiB of HBM per device.

```python
import math
import jax
import jax.numpy as jnp
from jax import lax

COMP = 5
FACES = 256
STEPS = 2
NP = 64
NS = 512


def touch_ends(drawn, rng, least, top_value):
    extent = drawn.shape
    spot = [jax.random.randint(jax.random.fold_in(rng, axis), (), 0, extent[axis]) for axis in range(len(extent))]
    drawn = drawn.at[tuple(spot)].set(least)
    longest = extent.index(max(extent))
    spot[longest] = (spot[longest] + 1) % extent[longest]
    return drawn.at[tuple(spot)].set(top_value)


def shard_levels(stream_key, shape, shards, least, high):
    level = 1.0
    for position, shards_of in shards:
        steps = jax.random.uniform(jax.random.fold_in(jax.random.fold_in(stream_key, 6), position), (shards_of,), jnp.float32, least / len(shards), high / len(shards))
        level = level * jnp.repeat(jnp.exp(steps), shape[position] // shards_of).reshape((-1,) + (1,) * (len(shape) - 1 - position))
    return level


def gaussian(stream_key, extent, scale, limit, pieces=(), held_as=jnp.bfloat16):
    drawn = scale * jax.random.normal(stream_key, extent, jnp.float32)
    if pieces:
        drawn = drawn * shard_levels(stream_key, extent, pieces, -0.22, 0.18)
    return jnp.clip(drawn, -limit, limit).astype(held_as)


def setup_inputs(seed: int = 0) -> dict:
    arg_keys = jax.random.split(jax.random.key(seed), 11)
    return {
        "stator_adj": gaussian(arg_keys[0], (COMP, NP, FACES, NS), 1.0, 6.0, ((1, 64), (3, 4)), jnp.float32),
        "rotor_adj": gaussian(arg_keys[1], (COMP, NP, FACES, NS), 1.0, 6.0, ((1, 64), (3, 4)), jnp.float32),
        "stator_rhs": gaussian(arg_keys[2], (COMP, NP, FACES, NS), 1.0, 6.0, ((1, 64), (3, 4)), jnp.float32),
        "rotor_rhs": gaussian(arg_keys[3], (COMP, NP, FACES, NS), 1.0, 6.0, ((1, 64), (3, 4)), jnp.float32),
        "stator_dtau": jnp.clip(jnp.exp(math.log(0.5) - 2.3025851 * jax.random.uniform(arg_keys[4], (NP, FACES, NS), jnp.float32) ** shard_levels(arg_keys[4], (NP, FACES, NS), ((0, 64), (2, 4)), -0.2, 0.2)), 0.05, 0.5),
        "rotor_dtau": jnp.clip(jnp.exp(math.log(0.5) - 2.3025851 * jax.random.uniform(arg_keys[5], (NP, FACES, NS), jnp.float32) ** shard_levels(arg_keys[5], (NP, FACES, NS), ((0, 64), (2, 4)), -0.2, 0.2)), 0.05, 0.5),
        "roe_jac": gaussian(arg_keys[6], (COMP, COMP, NP, FACES, NS), 0.4, 2.5, ((2, 64), (4, 4))),
        "pair_index": touch_ends(jax.random.randint(arg_keys[7], (2, NP, FACES), 0, 2 * FACES), jax.random.fold_in(arg_keys[7], 1), 0, (2 * FACES) - 1).astype(jnp.int32),
        "pair_weight": jnp.clip(0.1 + 0.9 * jax.random.uniform(arg_keys[8], (2, NP, FACES), jnp.float32) ** shard_levels(arg_keys[8], (2, NP, FACES), ((1, 64),), -0.2, 0.2), 0.1, 1.0),
        "rot_steps": jax.random.randint(arg_keys[9], (STEPS,), 0, NP).astype(jnp.int32),
    }


span_coupling = 0.25


def span_laplace(field):
    padded = jnp.pad(field, ((0, 0), (0, 0), (0, 0), (1, 1)))
    return padded[..., 2:] + padded[..., :-2] - 2.0 * field


def reference(stator_adj, rotor_adj, stator_rhs, rotor_rhs, stator_dtau, rotor_dtau, roe_jac, pair_index, pair_weight, rot_steps):
    columns = jnp.arange(2 * FACES, dtype=jnp.int32)
    intersection = jnp.sum(pair_weight[:, :, :, None] * (pair_index[:, :, :, None] == columns).astype(jnp.float32), axis=0)
    stator = stator_adj
    rotor = rotor_adj
    for pseudo in range(STEPS):
        rotation = rot_steps[pseudo]
        lower_strip = jnp.roll(rotor, rotation + 1, axis=1)
        upper_strip = jnp.roll(rotor, rotation, axis=1)
        paired = jnp.concatenate([lower_strip, upper_strip], axis=2)
        interp = jnp.einsum('jmk,cjks->cjms', intersection, paired, precision=lax.Precision.HIGHEST)
        flux_term = jnp.zeros_like(interp)
        for comp_in in range(COMP):
            flux_term = flux_term + roe_jac[comp_in].astype(jnp.float32) * interp[comp_in][None]
        credit = jnp.einsum('jmk,cjms->cjks', intersection, flux_term, precision=lax.Precision.HIGHEST)
        returned = jnp.roll(credit[:, :, FACES:], -rotation, axis=1) + jnp.roll(credit[:, :, :FACES], -rotation - 1, axis=1)
        new_stator = stator + stator_dtau * (stator_rhs - stator + span_coupling * span_laplace(stator) - flux_term)
        new_rotor = rotor + rotor_dtau * (rotor_rhs - rotor + span_coupling * span_laplace(rotor) + returned)
        stator, rotor = new_stator, new_rotor
    return stator, rotor
```

```python
import jax
import jax.numpy as jnp
from jax import lax
from jax.sharding import PartitionSpec as P

COMP = 5
STEPS = 2


span_coupling = 0.25


def from_behind(block, axis, distance):
    devices = range(lax.axis_size(axis))
    route = [((i - distance) % len(devices), i) for i in devices]
    return lax.ppermute(block, axis, route)


def padded_2(cells, sides, width):
    for axis, dim in sides:
        count = lax.axis_size(axis)
        ends = count - 1
        head = lax.slice_in_dim(cells, 0, width, axis=dim)
        tail = lax.slice_in_dim(cells, cells.shape[dim] - width, cells.shape[dim], axis=dim)
        cells = jnp.concatenate(
            [
                lax.ppermute(tail, axis, [(i, (i + 1) % count) for i in range(ends)]),
                cells,
                lax.ppermute(head, axis, [((i + 1) % count, i) for i in range(ends)]),
            ],
            axis=dim,
        )
    return cells


def rotated(block, amount, sign):
    cycle = lax.axis_size("pitch")

    def by(distance):
        return lambda held: from_behind(held, "pitch", sign * distance)

    return lax.switch(amount, [by(distance) for distance in range(cycle)], block)


def shards(
    stator_adj,
    rotor_adj,
    stator_rhs,
    rotor_rhs,
    stator_dtau,
    rotor_dtau,
    roe_jac,
    pair_index,
    pair_weight,
    rot_steps,
):
    face_count = stator_adj.shape[2]
    columns = jnp.arange(2 * face_count, dtype=jnp.int32)
    intersection = jnp.sum(
        pair_weight[:, :, :, None] * (pair_index[:, :, :, None] == columns).astype(jnp.float32),
        axis=0,
    )
    stator = stator_adj
    rotor = rotor_adj
    for pseudo in range(STEPS):
        rotation = rot_steps[pseudo]
        upper = rotated(rotor, rotation, 1)
        paired = jnp.concatenate([from_behind(upper, "pitch", 1), upper], axis=2)
        interp = jnp.einsum("jmk,cjks->cjms", intersection, paired, precision=lax.Precision.HIGHEST)
        flux_term = jnp.zeros_like(interp)
        for comp_in in range(COMP):
            flux_term = flux_term + roe_jac[comp_in].astype(jnp.float32) * interp[comp_in][None]
        credit = jnp.einsum(
            "jmk,cjms->cjks", intersection, flux_term, precision=lax.Precision.HIGHEST
        )
        shared = from_behind(credit[:, :, :face_count], "pitch", -1)
        returned = rotated(credit[:, :, face_count:] + shared, rotation, -1)
        stacked = jnp.stack([stator, rotor])
        padded = padded_2(stacked, (("span", 4),), 1)
        laplace = padded[..., 2:] + padded[..., :-2] - 2.0 * stacked
        new_stator = stator + stator_dtau * (
            stator_rhs - stator + span_coupling * laplace[0] - flux_term
        )
        new_rotor = rotor + rotor_dtau * (rotor_rhs - rotor + span_coupling * laplace[1] + returned)
        stator, rotor = (new_stator, new_rotor)
    return (stator, rotor)


def solution(mesh):
    in_specs = (
        P(None, "pitch", None, "span"),
        P(None, "pitch", None, "span"),
        P(None, "pitch", None, "span"),
        P(None, "pitch", None, "span"),
        P("pitch", None, "span"),
        P("pitch", None, "span"),
        P(None, None, "pitch", None, "span"),
        P(None, "pitch", None),
        P(None, "pitch", None),
        P(),
    )
    out_specs = (P(None, "pitch", None, "span"), P(None, "pitch", None, "span"))
    return jax.shard_map(shards, mesh=mesh, in_specs=in_specs, out_specs=out_specs, check_vma=False)
```

```python
import functools

import jax
import jax.numpy as jnp
from jax import lax
from jax.experimental import pallas as pl
from jax.experimental.pallas import tpu as pltpu
from jax.sharding import PartitionSpec as P

COMP = 5
STEPS = 2
LANES = 4
span_coupling = 0.25
MESH = pl.DeviceIdType.MESH

HOME_PLANES, HOME_LANES = 0, 1
OUT_PLANES, OUT_LANES, BACK_LANES, BACK_PLANES = 2, 3, 4, 5
END_LANES, END_PLANES = 10, 11
EDGES = 12
STAGES = 13
FIELDS = 2 * COMP + 1


def kernel(
    planes,
    sections,
    rot_ref,
    index_ref,
    weight_ref,
    stator_ref,
    rotor_ref,
    stator_rhs_ref,
    rotor_rhs_ref,
    stator_dtau_ref,
    rotor_dtau_ref,
    jac_ref,
    stator_out,
    rotor_out,
    home_in,
    home_split,
    spread,
    state,
    rolled,
    base,
    relay,
    packed,
    pair_in,
    interp,
    flux,
    credit_out,
    credit_in,
    sums,
    sums_in,
    summed,
    end_split,
    end_in,
    end_rows,
    edge_out,
    edge_in,
    weights,
    weights_t,
    send_sem,
    recv_sem,
):
    faces = stator_ref.shape[1]
    span = stator_ref.shape[2]
    strips = planes * LANES
    quarter = faces // LANES
    halves = planes // 2
    rows = faces // planes

    me = lax.axis_index("pitch")
    section = lax.axis_index("span")
    plane, lane = me // LANES, lax.rem(me, LANES)
    other_planes = [lax.rem(plane + d, planes) for d in range(1, planes)]
    other_lanes = [lax.rem(lane + d, LANES) for d in range(1, LANES)]
    left, right = lax.rem(section + sections - 1, sections), lax.rem(section + 1, sections)

    def eight(i):
        return pl.ds(pl.multiple_of(8 * i, 8), 8)

    def copy_to(src, dst, stage, n, target):
        pltpu.make_async_remote_copy(
            src, dst, send_sem.at[stage, n], recv_sem.at[stage, n], device_id=target, device_id_type=MESH
        ).start()

    def to_planes(src, dst, stage, n):
        for p in other_planes:
            copy_to(src(p), dst, stage, n, {"pitch": p * LANES + lane})

    def to_lanes(src, dst, stage, n):
        for y in other_lanes:
            copy_to(src(y), dst, stage, n, {"pitch": plane * LANES + y})

    finish = []

    def arrived(buf, stage, n):
        pltpu.make_async_copy(buf, buf, recv_sem.at[stage, n]).wait()
        finish.append((buf, stage, n))

    barrier = pltpu.get_barrier_semaphore()
    for p in other_planes:
        pl.semaphore_signal(barrier, inc=1, device_id={"pitch": p * LANES + lane}, device_id_type=MESH)
    for y in other_lanes:
        pl.semaphore_signal(barrier, inc=1, device_id={"pitch": plane * LANES + y}, device_id_type=MESH)
    for t in (left, right):
        pl.semaphore_signal(barrier, inc=1, device_id={"span": t}, device_id_type=MESH)
    pl.semaphore_wait(barrier, planes - 1 + LANES - 1 + 2)

    def field(n):
        if n < COMP:
            return rotor_ref.at[n]
        if n < 2 * COMP:
            return rotor_rhs_ref.at[n - COMP]
        return rotor_dtau_ref

    def send_home(n):
        src = field(n)

        def part(p):
            return src.at[pl.ds(pl.multiple_of(p * rows, rows), rows)]

        to_planes(part, home_in.at[n, plane], HOME_PLANES, n)
        home_in[n, plane] = src[pl.ds(pl.multiple_of(plane * rows, rows), rows)]

    def split_home(n):
        arrived(home_in.at[n, pl.ds(0, planes - 1)], HOME_PLANES, n)

        def body(i, carry):
            one, two = home_in[n, 2 * i], home_in[n, 2 * i + 1]
            for y in range(LANES):
                home_split[n, y, eight(i)] = jnp.concatenate([one[4 * y : 4 * y + 4], two[4 * y : 4 * y + 4]], axis=0)
            return carry

        lax.fori_loop(0, halves, body, 0)
        to_lanes(lambda y: home_split.at[n, y], spread.at[n, lane], HOME_LANES, n)
        spread[n, lane] = home_split[n, lane]

    def spread_here(n):
        arrived(spread.at[n, pl.ds(0, LANES - 1)], HOME_LANES, n)

    def send_strips(step, c):
        rotation = rot_ref[step]
        places = []
        for b in range(LANES):
            offset = (b - 1 - rotation + 2 * strips) & (strips - 1)
            places.append((offset & (LANES - 1), offset >> 2))

        def body(a, carry):
            for b, (y, q) in enumerate(places):
                rolled[step, c, LANES * a + b] = state[step, c, y, (a + q) & (planes - 1)]
            return carry

        lax.fori_loop(0, planes, body, 0)
        rolled[step, c, strips] = state[step, c, places[0][0], places[0][1]]

        def part(p):
            return rolled.at[step, c, pl.ds(p * LANES, LANES + 1)]

        to_planes(part, relay.at[step, c, plane], OUT_PLANES + 4 * step, c)
        relay[step, c, plane] = rolled[step, c, pl.ds(plane * LANES, LANES + 1)]

    def first_state(c):
        def body(i, carry):
            for y in range(LANES):
                held = spread[c, y, eight(i)]
                state[0, c, y, 2 * i] = held[:4]
                state[0, c, y, 2 * i + 1] = held[4:]
            return carry

        lax.fori_loop(0, halves, body, 0)

    def pack(step, c):
        arrived(relay.at[step, c, pl.ds(0, planes - 1)], OUT_PLANES + 4 * step, c)

        def body(i, carry):
            for u in range(LANES + 1):
                packed[step, c, u, eight(i)] = jnp.concatenate(
                    [relay[step, c, 2 * i, u], relay[step, c, 2 * i + 1, u]], axis=0
                )
            return carry

        lax.fori_loop(0, halves, body, 0)
        to_lanes(
            lambda y: packed.at[step, c, pl.ds(y, 2)], pair_in.at[step, c, lane], OUT_LANES + 4 * step, c
        )
        pair_in[step, c, lane] = packed[step, c, pl.ds(lane, 2)]

    def split(x):
        high = x.astype(jnp.bfloat16)
        return high, (x - high.astype(jnp.float32)).astype(jnp.bfloat16)

    def product(table, x):
        high, low = split(x)
        total = jnp.dot(table[0], high, preferred_element_type=jnp.float32)
        total += jnp.dot(table[1], high, preferred_element_type=jnp.float32)
        return total + jnp.dot(table[0], low, preferred_element_type=jnp.float32)

    def build_weights():
        place = lax.broadcasted_iota(jnp.int32, (2 * faces, faces), 0)
        half, inner = place // faces, lax.rem(place, faces)
        y, inner = inner // quarter, lax.rem(inner, quarter)
        face = half * faces + (inner // 4) * rows + 4 * y + lax.rem(inner, 4)
        table = jnp.zeros((2 * faces, faces), jnp.float32)
        for p in range(2):
            table += jnp.where(index_ref[p : p + 1] == face, weight_ref[p : p + 1], 0.0)
        weights_t[0], weights_t[1] = split(table)
        weights[0], weights[1] = split(table.T)

    def interpolate(step, c):
        arrived(pair_in.at[step, c, pl.ds(0, LANES - 1)], OUT_LANES + 4 * step, c)
        paired = jnp.concatenate([pair_in[step, c, y, h] for h in range(2) for y in range(LANES)], axis=0)
        interp[c] = product(weights, paired)

    def flux_and_credit(step, b):
        total = jac_ref[0, b].astype(jnp.float32) * interp[0]
        for a in range(1, COMP):
            total += jac_ref[a, b].astype(jnp.float32) * interp[a]
        flux[b] = total
        credit = product(weights_t, total)
        for h in range(2):
            for y in range(LANES):
                start = h * faces + y * quarter
                credit_out[step, b, y, h] = credit[start : start + quarter]
        to_lanes(
            lambda y: credit_out.at[step, b, y], credit_in.at[step, b, lane], BACK_LANES + 4 * step, b
        )
        credit_in[step, b, lane] = credit_out[step, b, lane]

    def sum_credit(step, b):
        arrived(credit_in.at[step, b, pl.ds(0, LANES - 1)], BACK_LANES + 4 * step, b)

        def body(i, carry):
            for u in range(LANES + 1):
                if u == 0:
                    total = credit_in[step, b, 0, 0, eight(i)]
                elif u == LANES:
                    total = credit_in[step, b, LANES - 1, 1, eight(i)]
                else:
                    total = credit_in[step, b, u, 0, eight(i)] + credit_in[step, b, u - 1, 1, eight(i)]
                sums[step, b, 2 * i, u] = total[:4]
                sums[step, b, 2 * i + 1, u] = total[4:]
            return carry

        lax.fori_loop(0, halves, body, 0)
        to_planes(lambda p: sums.at[step, b, p], sums_in.at[step, b, plane], BACK_PLANES + 4 * step, b)
        sums_in[step, b, plane] = sums[step, b, plane]

    def update(step, b):
        rotation = rot_ref[step]
        arrived(sums_in.at[step, b, pl.ds(0, planes - 1)], BACK_PLANES + 4 * step, b)

        def gather(p, carry):
            for v in range(LANES - 1):
                summed[v, p] = sums_in[step, b, p, v + 1]
            after = (p + 1) & (planes - 1)
            summed[LANES - 1, p] = sums_in[step, b, p, LANES] + sums_in[step, b, after, 0]
            return carry

        lax.fori_loop(0, planes, gather, 0)
        places = []
        for y in range(LANES):
            offset = (y + rotation) & (strips - 1)
            places.append((offset & (LANES - 1), offset >> 2))

        def body(i, carry):
            for y, (v, q) in enumerate(places):
                first, second = (q + 2 * i) & (planes - 1), (q + 2 * i + 1) & (planes - 1)
                returned = jnp.concatenate([summed[v, first], summed[v, second]], axis=0)
                new = base[step, b, y, eight(i)] + spread[2 * COMP, y, eight(i)] * returned
                if step == 0:
                    state[1, b, y, 2 * i] = new[:4]
                    state[1, b, y, 2 * i + 1] = new[4:]
                    spread[b, y, eight(i)] = new
                else:
                    end_split[b, y, eight(i)] = new
            return carry

        lax.fori_loop(0, halves, body, 0)

    def send_edges(n, fetch):
        row = lax.broadcasted_iota(jnp.int32, (8, span), 0)
        col = lax.broadcasted_iota(jnp.int32, (8, span), 1)
        pick = ((row == 0) & (col == 0)) | ((row == 1) & (col == span - 1))
        pick = jnp.where(pick, 1.0, 0.0).astype(jnp.float32)
        for c in range(COMP):
            edge_out[n, c] = lax.dot_general(
                pick, fetch(c), (((1,), (1,)), ((), ())),
                precision=lax.Precision.HIGHEST, preferred_element_type=jnp.float32,
            )
        copy_to(edge_out.at[n], edge_in.at[n, 0], EDGES, 2 * n, {"span": right})
        copy_to(edge_out.at[n], edge_in.at[n, 1], EDGES, 2 * n + 1, {"span": left})

    def edges_here(n):
        arrived(edge_in.at[n, 0], EDGES, 2 * n)
        arrived(edge_in.at[n, 1], EDGES, 2 * n + 1)

    def laplace(n, c, x):
        row = lax.broadcasted_iota(jnp.int32, (16, span), 0)
        col = lax.broadcasted_iota(jnp.int32, (16, span), 1)
        place = ((row == 1) & (col == 0) & (section > 0)) | (
            (row == 8) & (col == span - 1) & (section < sections - 1)
        )
        place = jnp.where(place, 1.0, 0.0).astype(jnp.float32)
        held = jnp.concatenate([edge_in[n, 0, c], edge_in[n, 1, c]], axis=0)
        beyond = lax.dot_general(
            held, place, (((0,), (0,)), ((), ())),
            precision=lax.Precision.HIGHEST, preferred_element_type=jnp.float32,
        )
        at = lax.broadcasted_iota(jnp.int32, x.shape, 1)
        before = jnp.where(at == 0, 0.0, pltpu.roll(x, 1, 1))
        after = jnp.where(at == span - 1, 0.0, pltpu.roll(x, span - 1, 1))
        return before + after + beyond - 2.0 * x

    def spread_field(n):
        return spread[n].reshape(faces, span)

    def build_base(step, c):
        x = spread_field(c)
        change = spread_field(COMP + c) - x + span_coupling * laplace(1 + step, c, x)
        base[step, c] = (x + spread_field(2 * COMP) * change).reshape(LANES, quarter, span)

    def stator_step(step, c):
        source = stator_ref if step == 0 else stator_out
        x = source[c]
        change = stator_rhs_ref[c] - x + span_coupling * laplace(3 * step, c, x) - flux[c]
        stator_out[c] = x + stator_dtau_ref[...] * change

    def send_end(c):
        to_lanes(lambda y: end_split.at[c, y], end_in.at[c, lane], END_LANES, c)
        end_in[c, lane] = end_split[c, lane]

    def join_end(c):
        arrived(end_in.at[c, pl.ds(0, LANES - 1)], END_LANES, c)

        def body(i, carry):
            held = [end_in[c, y, eight(i)] for y in range(LANES)]
            end_rows[c, 2 * i] = jnp.concatenate([h[:4] for h in held], axis=0)
            end_rows[c, 2 * i + 1] = jnp.concatenate([h[4:] for h in held], axis=0)
            return carry

        lax.fori_loop(0, halves, body, 0)
        mine = pl.ds(pl.multiple_of(plane * rows, rows), rows)
        to_planes(lambda p: end_rows.at[c, p], rotor_out.at[c, mine], END_PLANES, c)
        rotor_out[c, mine] = end_rows[c, plane]

    every = range(COMP)
    for c in every:
        send_home(c)
    send_edges(0, lambda c: stator_ref[c])
    build_weights()

    def take(c):
        spread_here(c)
        first_state(c)
        send_strips(0, c)

    for c in every:
        split_home(c)
        if c:
            take(c - 1)
    take(COMP - 1)
    send_edges(1, spread_field)
    for c in every:
        pack(0, c)
        if c:
            interpolate(0, c - 1)
    for n in [2 * COMP] + list(range(COMP, 2 * COMP)):
        send_home(n)
    interpolate(0, COMP - 1)
    for b in every:
        flux_and_credit(0, b)
    edges_here(0)
    for n in [2 * COMP] + list(range(COMP, 2 * COMP)):
        split_home(n)
    for b in every:
        sum_credit(0, b)
    for c in every:
        stator_step(0, c)
    send_edges(3, lambda c: stator_out[c])
    edges_here(1)
    spread_here(2 * COMP)
    for b in every:
        spread_here(COMP + b)
        build_base(0, b)
        update(0, b)
        send_strips(1, b)
    send_edges(2, spread_field)
    for c in every:
        pack(1, c)
        if c:
            interpolate(1, c - 1)
    interpolate(1, COMP - 1)
    for b in every:
        flux_and_credit(1, b)
    edges_here(2)
    for c in every:
        build_base(1, c)
    for b in every:
        sum_credit(1, b)
    edges_here(3)
    for c in every:
        stator_step(1, c)
    for b in every:
        update(1, b)
        send_end(b)
        if b:
            join_end(b - 1)
    join_end(COMP - 1)
    for c in every:
        arrived(rotor_out.at[c, pl.ds(0, (planes - 1) * rows)], END_PLANES, c)
    for buf, stage, n in finish:
        pltpu.make_async_copy(buf, buf, send_sem.at[stage, n]).wait()


def shards(
    stator_adj,
    rotor_adj,
    stator_rhs,
    rotor_rhs,
    stator_dtau,
    rotor_dtau,
    roe_jac,
    pair_index,
    pair_weight,
    rot_steps,
):
    _, _, faces, span = stator_adj.shape
    planes = lax.axis_size("pitch") // LANES
    sections = lax.axis_size("span")
    quarter, rows = faces // LANES, faces // planes
    f32, bf16 = jnp.float32, jnp.bfloat16
    vmem = pl.BlockSpec(memory_space=pltpu.VMEM)
    out = jax.ShapeDtypeStruct((COMP, faces, span), f32)
    strips = planes * LANES
    scratch = [
        pltpu.VMEM((FIELDS, planes, rows, span), f32),
        pltpu.VMEM((FIELDS, LANES, quarter, span), f32),
        pltpu.VMEM((FIELDS, LANES, quarter, span), f32),
        pltpu.VMEM((STEPS, COMP, LANES, planes, 4, span), f32),
        pltpu.VMEM((STEPS, COMP, strips + 1, 4, span), f32),
        pltpu.VMEM((STEPS, COMP, LANES, quarter, span), f32),
        pltpu.VMEM((STEPS, COMP, planes, LANES + 1, 4, span), f32),
        pltpu.VMEM((STEPS, COMP, LANES + 1, quarter, span), f32),
        pltpu.VMEM((STEPS, COMP, LANES, 2, quarter, span), f32),
        pltpu.VMEM((COMP, faces, span), f32),
        pltpu.VMEM((COMP, faces, span), f32),
        pltpu.VMEM((STEPS, COMP, LANES, 2, quarter, span), f32),
        pltpu.VMEM((STEPS, COMP, LANES, 2, quarter, span), f32),
        pltpu.VMEM((STEPS, COMP, planes, LANES + 1, 4, span), f32),
        pltpu.VMEM((STEPS, COMP, planes, LANES + 1, 4, span), f32),
        pltpu.VMEM((LANES, planes, 4, span), f32),
        pltpu.VMEM((COMP, LANES, quarter, span), f32),
        pltpu.VMEM((COMP, LANES, quarter, span), f32),
        pltpu.VMEM((COMP, planes, rows, span), f32),
        pltpu.VMEM((4, COMP, 8, faces), f32),
        pltpu.VMEM((4, 2, COMP, 8, faces), f32),
        pltpu.VMEM((2, faces, 2 * faces), bf16),
        pltpu.VMEM((2, 2 * faces, faces), bf16),
        pltpu.SemaphoreType.DMA((STAGES, FIELDS)),
        pltpu.SemaphoreType.DMA((STAGES, FIELDS)),
    ]
    stator, rotor = pl.pallas_call(
        functools.partial(kernel, planes, sections),
        out_shape=(out, out),
        in_specs=[pl.BlockSpec(memory_space=pltpu.SMEM)] + [vmem] * 9,
        out_specs=(vmem, vmem),
        scratch_shapes=scratch,
        compiler_params=pltpu.CompilerParams(
            collective_id=0, has_side_effects=True, vmem_limit_bytes=60 * 1024 * 1024
        ),
        name="sliding_interface",
    )(
        rot_steps,
        pair_index[:, 0],
        pair_weight[:, 0],
        stator_adj[:, 0],
        rotor_adj[:, 0],
        stator_rhs[:, 0],
        rotor_rhs[:, 0],
        stator_dtau[0],
        rotor_dtau[0],
        roe_jac[:, :, 0],
    )
    return stator[:, None], rotor[:, None]


def solution(mesh):
    in_specs = (
        P(None, "pitch", None, "span"),
        P(None, "pitch", None, "span"),
        P(None, "pitch", None, "span"),
        P(None, "pitch", None, "span"),
        P("pitch", None, "span"),
        P("pitch", None, "span"),
        P(None, None, "pitch", None, "span"),
        P(None, "pitch", None),
        P(None, "pitch", None),
        P(),
    )
    out_specs = (P(None, "pitch", None, "span"), P(None, "pitch", None, "span"))
    return jax.shard_map(shards, mesh=mesh, in_specs=in_specs, out_specs=out_specs, check_vma=False)
```

```python
import functools

import jax
import jax.numpy as jnp
from jax import lax
from jax.experimental import pallas as pl
from jax.experimental.pallas import tpu as pltpu
from jax.sharding import PartitionSpec as P

COMP = 5
STEPS = 2
LANES = 4
span_coupling = 0.25
MESH = pl.DeviceIdType.MESH

HOME_PLANES, HOME_LANES = 0, 1
OUT_PLANES, OUT_LANES, BACK_LANES, BACK_PLANES = 2, 3, 4, 5
END_LANES, END_PLANES = 10, 11
EDGES = 12
LOCAL = 13
STAGES = 14
FIELDS = 2 * COMP + 1


def kernel(
    planes,
    sections,
    rot_ref,
    index_ref,
    weight_ref,
    stator_hbm,
    rotor_hbm,
    stator_rhs_hbm,
    rotor_rhs_hbm,
    stator_dtau_hbm,
    rotor_dtau_hbm,
    jac_hbm,
    stator_out,
    rotor_out,
    stator_ref,
    stator_rhs_ref,
    stator_dtau_ref,
    jac_ref,
    home_in,
    home_split,
    spread,
    state,
    rolled,
    base,
    relay,
    packed,
    pair_in,
    interp,
    flux,
    credit_out,
    credit_in,
    sums,
    sums_in,
    summed,
    end_split,
    end_in,
    end_rows,
    edge_out,
    edge_in,
    weights,
    weights_t,
    send_sem,
    recv_sem,
):
    faces, span = stator_ref.shape[1:]
    strips = planes * LANES
    quarter = faces // LANES
    halves = planes // 2
    rows = faces // planes

    me = lax.axis_index("pitch")
    section = lax.axis_index("span")
    plane, lane = me // LANES, lax.rem(me, LANES)
    other_planes = [lax.rem(plane + d, planes) for d in range(1, planes)]
    other_lanes = [lax.rem(lane + d, LANES) for d in range(1, LANES)]
    left, right = lax.rem(section + sections - 1, sections), lax.rem(section + 1, sections)

    def eight(i):
        return pl.ds(pl.multiple_of(8 * i, 8), 8)

    def copy_to(src, dst, stage, n, target):
        pltpu.make_async_remote_copy(
            src, dst, send_sem.at[stage, n], recv_sem.at[stage, n], device_id=target, device_id_type=MESH
        ).start()

    def to_planes(src, dst, stage, n):
        for p in other_planes:
            copy_to(src(p), dst, stage, n, {"pitch": p * LANES + lane})

    def to_lanes(src, dst, stage, n):
        for y in other_lanes:
            copy_to(src(y), dst, stage, n, {"pitch": plane * LANES + y})

    finish = []

    def wait(buf, stage, n):
        pltpu.make_async_copy(buf, buf, recv_sem.at[stage, n]).wait()

    def arrived(buf, stage, n):
        wait(buf, stage, n)
        finish.append((buf, stage, n))

    def keep(src, dst, stage, n):
        pltpu.make_async_copy(src, dst, recv_sem.at[stage, n]).start()

    own = (
        (stator_hbm, stator_ref),
        (stator_dtau_hbm, stator_dtau_ref),
        (stator_rhs_hbm, stator_rhs_ref),
        (jac_hbm, jac_ref),
    )
    for n, (src, dst) in enumerate(own):
        keep(src, dst, LOCAL, n)

    def own_here(n):
        wait(own[n][1], LOCAL, n)

    barrier = pltpu.get_barrier_semaphore()
    for p in other_planes:
        pl.semaphore_signal(barrier, inc=1, device_id={"pitch": p * LANES + lane}, device_id_type=MESH)
    for y in other_lanes:
        pl.semaphore_signal(barrier, inc=1, device_id={"pitch": plane * LANES + y}, device_id_type=MESH)
    for t in (left, right):
        pl.semaphore_signal(barrier, inc=1, device_id={"span": t}, device_id_type=MESH)
    pl.semaphore_wait(barrier, planes - 1 + LANES - 1 + 2)

    def field(n):
        if n < COMP:
            return rotor_hbm.at[n]
        if n < 2 * COMP:
            return rotor_rhs_hbm.at[n - COMP]
        return rotor_dtau_hbm

    def send_home(n):
        src = field(n)

        def part(p):
            return src.at[pl.ds(pl.multiple_of(p * rows, rows), rows)]

        to_planes(part, home_in.at[n, plane], HOME_PLANES, n)
        keep(part(plane), home_in.at[n, plane], HOME_PLANES, n)

    def split_home(n):
        wait(home_in.at[n], HOME_PLANES, n)
        finish.append((home_in.at[n, pl.ds(0, planes - 1)], HOME_PLANES, n))

        def body(i, carry):
            one, two = home_in[n, 2 * i], home_in[n, 2 * i + 1]
            for y in range(LANES):
                home_split[n, y, eight(i)] = jnp.concatenate([one[4 * y : 4 * y + 4], two[4 * y : 4 * y + 4]], axis=0)
            return carry

        lax.fori_loop(0, halves, body, 0)
        to_lanes(lambda y: home_split.at[n, y], spread.at[n, lane], HOME_LANES, n)
        spread[n, lane] = home_split[n, lane]

    def spread_here(n):
        arrived(spread.at[n, pl.ds(0, LANES - 1)], HOME_LANES, n)

    def send_strips(step, c):
        rotation = rot_ref[step]
        places = []
        for b in range(LANES):
            offset = (b - 1 - rotation + 2 * strips) & (strips - 1)
            places.append((offset & (LANES - 1), offset >> 2))

        def body(a, carry):
            for b, (y, q) in enumerate(places):
                rolled[step, c, LANES * a + b] = state[step, c, y, (a + q) & (planes - 1)]
            return carry

        lax.fori_loop(0, planes, body, 0)
        rolled[step, c, strips] = state[step, c, places[0][0], places[0][1]]

        def part(p):
            return rolled.at[step, c, pl.ds(p * LANES, LANES + 1)]

        to_planes(part, relay.at[step, c, plane], OUT_PLANES + 4 * step, c)
        relay[step, c, plane] = rolled[step, c, pl.ds(plane * LANES, LANES + 1)]

    def first_state(c):
        def body(i, carry):
            for y in range(LANES):
                held = spread[c, y, eight(i)]
                state[0, c, y, 2 * i] = held[:4]
                state[0, c, y, 2 * i + 1] = held[4:]
            return carry

        lax.fori_loop(0, halves, body, 0)

    def pack(step, c):
        arrived(relay.at[step, c, pl.ds(0, planes - 1)], OUT_PLANES + 4 * step, c)

        def body(i, carry):
            for u in range(LANES + 1):
                packed[step, c, u, eight(i)] = jnp.concatenate(
                    [relay[step, c, 2 * i, u], relay[step, c, 2 * i + 1, u]], axis=0
                )
            return carry

        lax.fori_loop(0, halves, body, 0)
        to_lanes(
            lambda y: packed.at[step, c, pl.ds(y, 2)], pair_in.at[step, c, lane], OUT_LANES + 4 * step, c
        )
        pair_in[step, c, lane] = packed[step, c, pl.ds(lane, 2)]

    def split(x):
        high = x.astype(jnp.bfloat16)
        return high, (x - high.astype(jnp.float32)).astype(jnp.bfloat16)

    def product(table, x):
        high, low = split(x)
        total = jnp.dot(table[0], high, preferred_element_type=jnp.float32)
        total += jnp.dot(table[1], high, preferred_element_type=jnp.float32)
        return total + jnp.dot(table[0], low, preferred_element_type=jnp.float32)

    def build_weights():
        place = lax.broadcasted_iota(jnp.int32, (2 * faces, faces), 0)
        half, inner = place // faces, lax.rem(place, faces)
        y, inner = inner // quarter, lax.rem(inner, quarter)
        face = half * faces + (inner // 4) * rows + 4 * y + lax.rem(inner, 4)
        table = jnp.zeros((2 * faces, faces), jnp.float32)
        for p in range(2):
            table += jnp.where(index_ref[p] == face, weight_ref[p], 0.0)
        weights_t[0], weights_t[1] = split(table)
        weights[0], weights[1] = split(table.T)

    def interpolate(step, c):
        arrived(pair_in.at[step, c, pl.ds(0, LANES - 1)], OUT_LANES + 4 * step, c)
        paired = jnp.concatenate([pair_in[step, c, y, h] for h in range(2) for y in range(LANES)], axis=0)
        value = product(weights, paired)
        interp[c] = value
        if c < COMP - 1:
            for b in range(COMP):
                term = jac_ref[c, b].astype(jnp.float32) * value
                flux[b] = flux[b] + term if c else term

    def flux_and_credit(step, b):
        total = flux[b] + jac_ref[COMP - 1, b].astype(jnp.float32) * interp[COMP - 1]
        flux[b] = total
        credit = product(weights_t, total)
        for h in range(2):
            for y in range(LANES):
                start = h * faces + y * quarter
                credit_out[step, b, y, h] = credit[start : start + quarter]
        to_lanes(
            lambda y: credit_out.at[step, b, y], credit_in.at[step, b, lane], BACK_LANES + 4 * step, b
        )
        credit_in[step, b, lane] = credit_out[step, b, lane]

    def sum_credit(step, b):
        arrived(credit_in.at[step, b, pl.ds(0, LANES - 1)], BACK_LANES + 4 * step, b)

        def body(i, carry):
            for u in range(LANES + 1):
                if u == 0:
                    total = credit_in[step, b, 0, 0, eight(i)]
                elif u == LANES:
                    total = credit_in[step, b, LANES - 1, 1, eight(i)]
                else:
                    total = credit_in[step, b, u, 0, eight(i)] + credit_in[step, b, u - 1, 1, eight(i)]
                sums[step, b, 2 * i, u] = total[:4]
                sums[step, b, 2 * i + 1, u] = total[4:]
            return carry

        lax.fori_loop(0, halves, body, 0)
        to_planes(lambda p: sums.at[step, b, p], sums_in.at[step, b, plane], BACK_PLANES + 4 * step, b)
        sums_in[step, b, plane] = sums[step, b, plane]

    def update(step, b):
        rotation = rot_ref[step]
        arrived(sums_in.at[step, b, pl.ds(0, planes - 1)], BACK_PLANES + 4 * step, b)

        def gather(p, carry):
            for v in range(LANES - 1):
                summed[v, p] = sums_in[step, b, p, v + 1]
            after = (p + 1) & (planes - 1)
            summed[LANES - 1, p] = sums_in[step, b, p, LANES] + sums_in[step, b, after, 0]
            return carry

        lax.fori_loop(0, planes, gather, 0)
        places = []
        for y in range(LANES):
            offset = (y + rotation) & (strips - 1)
            places.append((offset & (LANES - 1), offset >> 2))

        def body(i, carry):
            for y, (v, q) in enumerate(places):
                first, second = (q + 2 * i) & (planes - 1), (q + 2 * i + 1) & (planes - 1)
                returned = jnp.concatenate([summed[v, first], summed[v, second]], axis=0)
                new = base[step, b, y, eight(i)] + spread[2 * COMP, y, eight(i)] * returned
                if step == 0:
                    state[1, b, y, 2 * i] = new[:4]
                    state[1, b, y, 2 * i + 1] = new[4:]
                    spread[b, y, eight(i)] = new
                else:
                    end_split[b, y, eight(i)] = new
            return carry

        lax.fori_loop(0, halves, body, 0)

    def send_edges(n, fetch):
        row = lax.broadcasted_iota(jnp.int32, (8, span), 0)
        col = lax.broadcasted_iota(jnp.int32, (8, span), 1)
        pick = ((row == 0) & (col == 0)) | ((row == 1) & (col == span - 1))
        pick = jnp.where(pick, 1.0, 0.0).astype(jnp.float32)
        for c in range(COMP):
            edge_out[n, c] = lax.dot_general(
                pick, fetch(c), (((1,), (1,)), ((), ())),
                precision=lax.Precision.HIGHEST, preferred_element_type=jnp.float32,
            )
        copy_to(edge_out.at[n], edge_in.at[n, 0], EDGES, 2 * n, {"span": right})
        copy_to(edge_out.at[n], edge_in.at[n, 1], EDGES, 2 * n + 1, {"span": left})

    def edges_here(n):
        arrived(edge_in.at[n, 0], EDGES, 2 * n)
        arrived(edge_in.at[n, 1], EDGES, 2 * n + 1)

    def laplace(n, c, x):
        row = lax.broadcasted_iota(jnp.int32, (16, span), 0)
        col = lax.broadcasted_iota(jnp.int32, (16, span), 1)
        place = ((row == 1) & (col == 0) & (section > 0)) | (
            (row == 8) & (col == span - 1) & (section < sections - 1)
        )
        place = jnp.where(place, 1.0, 0.0).astype(jnp.float32)
        held = jnp.concatenate([edge_in[n, 0, c], edge_in[n, 1, c]], axis=0)
        beyond = lax.dot_general(
            held, place, (((0,), (0,)), ((), ())),
            precision=lax.Precision.HIGHEST, preferred_element_type=jnp.float32,
        )
        at = lax.broadcasted_iota(jnp.int32, x.shape, 1)
        before = jnp.where(at == 0, 0.0, pltpu.roll(x, 1, 1))
        after = jnp.where(at == span - 1, 0.0, pltpu.roll(x, span - 1, 1))
        return before + after + beyond - 2.0 * x

    def spread_field(n):
        return spread[n].reshape(faces, span)

    def build_base(step, c):
        x = spread_field(c)
        change = spread_field(COMP + c) - x + span_coupling * laplace(1 + step, c, x)
        base[step, c] = (x + spread_field(2 * COMP) * change).reshape(LANES, quarter, span)

    def stator_step(step, c):
        source = stator_ref if step == 0 else stator_out
        x = source[c]
        change = stator_rhs_ref[c] - x + span_coupling * laplace(3 * step, c, x) - flux[c]
        stator_out[c] = x + stator_dtau_ref[...] * change

    def send_end(c):
        to_lanes(lambda y: end_split.at[c, y], end_in.at[c, lane], END_LANES, c)
        end_in[c, lane] = end_split[c, lane]

    def join_end(c):
        arrived(end_in.at[c, pl.ds(0, LANES - 1)], END_LANES, c)

        def body(i, carry):
            held = [end_in[c, y, eight(i)] for y in range(LANES)]
            end_rows[c, 2 * i] = jnp.concatenate([h[:4] for h in held], axis=0)
            end_rows[c, 2 * i + 1] = jnp.concatenate([h[4:] for h in held], axis=0)
            return carry

        lax.fori_loop(0, halves, body, 0)
        mine = pl.ds(pl.multiple_of(plane * rows, rows), rows)
        to_planes(lambda p: end_rows.at[c, p], rotor_out.at[c, mine], END_PLANES, c)
        keep(end_rows.at[c, plane], rotor_out.at[c, mine], END_PLANES, c)

    every = range(COMP)
    late = [2 * COMP] + [COMP + c for c in every]

    def take(c):
        spread_here(c)
        first_state(c)
        send_strips(0, c)

    def to_stator(step):
        for c in every:
            pack(step, c)
            if c:
                interpolate(step, c - 1)
            if c == COMP - 1 and step == 0:
                for n in late[2:]:
                    send_home(n)
        interpolate(step, COMP - 1)

    def to_spread(step):
        for b in every:
            flux_and_credit(step, b)
            if b >= 2:
                sum_credit(step, b - 2)
        sum_credit(step, COMP - 2)
        sum_credit(step, COMP - 1)

    for c in every:
        send_home(c)
    own_here(0)
    send_edges(0, lambda c: stator_ref[c])
    build_weights()
    for c in every:
        split_home(c)
        if c < 2:
            send_home(late[c])
        if c:
            take(c - 1)
    take(COMP - 1)
    send_edges(1, spread_field)
    own_here(3)
    to_stator(0)
    to_spread(0)
    edges_here(0)
    own_here(1)
    own_here(2)
    for n in late[:2]:
        split_home(n)
    for c in every:
        stator_step(0, c)
    send_edges(3, lambda c: stator_out[c])
    edges_here(1)
    spread_here(2 * COMP)
    for b in every:
        if b < COMP - 1:
            split_home(late[b + 2])
        spread_here(COMP + b)
        build_base(0, b)
        update(0, b)
        send_strips(1, b)
    send_edges(2, spread_field)
    to_stator(1)
    to_spread(1)
    edges_here(2)
    for c in every:
        build_base(1, c)
    edges_here(3)
    for b in every:
        update(1, b)
        send_end(b)
        if b:
            join_end(b - 1)
    join_end(COMP - 1)
    for c in every:
        stator_step(1, c)
    for c in every:
        wait(rotor_out.at[c], END_PLANES, c)
        finish.append((rotor_out.at[c, pl.ds(0, (planes - 1) * rows)], END_PLANES, c))
    for buf, stage, n in finish:
        pltpu.make_async_copy(buf, buf, send_sem.at[stage, n]).wait()


def shards(
    stator_adj,
    rotor_adj,
    stator_rhs,
    rotor_rhs,
    stator_dtau,
    rotor_dtau,
    roe_jac,
    pair_index,
    pair_weight,
    rot_steps,
):
    _, _, faces, span = stator_adj.shape
    planes = lax.axis_size("pitch") // LANES
    sections = lax.axis_size("span")
    quarter, rows = faces // LANES, faces // planes
    f32, bf16 = jnp.float32, jnp.bfloat16
    vmem = pl.BlockSpec(memory_space=pltpu.VMEM)
    hbm = pl.BlockSpec(memory_space=pl.ANY)
    out = pltpu.VMEM((COMP, faces, span), f32)
    strips = planes * LANES
    scratch = [
        pltpu.VMEM((COMP, faces, span), f32),
        pltpu.VMEM((COMP, faces, span), f32),
        pltpu.VMEM((faces, span), f32),
        pltpu.VMEM((COMP, COMP, faces, span), bf16),
        pltpu.VMEM((FIELDS, planes, rows, span), f32),
        pltpu.VMEM((FIELDS, LANES, quarter, span), f32),
        pltpu.VMEM((FIELDS, LANES, quarter, span), f32),
        pltpu.VMEM((STEPS, COMP, LANES, planes, 4, span), f32),
        pltpu.VMEM((STEPS, COMP, strips + 1, 4, span), f32),
        pltpu.VMEM((STEPS, COMP, LANES, quarter, span), f32),
        pltpu.VMEM((STEPS, COMP, planes, LANES + 1, 4, span), f32),
        pltpu.VMEM((STEPS, COMP, LANES + 1, quarter, span), f32),
        pltpu.VMEM((STEPS, COMP, LANES, 2, quarter, span), f32),
        pltpu.VMEM((COMP, faces, span), f32),
        pltpu.VMEM((COMP, faces, span), f32),
        pltpu.VMEM((STEPS, COMP, LANES, 2, quarter, span), f32),
        pltpu.VMEM((STEPS, COMP, LANES, 2, quarter, span), f32),
        pltpu.VMEM((STEPS, COMP, planes, LANES + 1, 4, span), f32),
        pltpu.VMEM((STEPS, COMP, planes, LANES + 1, 4, span), f32),
        pltpu.VMEM((LANES, planes, 4, span), f32),
        pltpu.VMEM((COMP, LANES, quarter, span), f32),
        pltpu.VMEM((COMP, LANES, quarter, span), f32),
        pltpu.VMEM((COMP, planes, rows, span), f32),
        pltpu.VMEM((4, COMP, 8, faces), f32),
        pltpu.VMEM((4, 2, COMP, 8, faces), f32),
        pltpu.VMEM((2, faces, 2 * faces), bf16),
        pltpu.VMEM((2, 2 * faces, faces), bf16),
        pltpu.SemaphoreType.DMA((STAGES, FIELDS)),
        pltpu.SemaphoreType.DMA((STAGES, FIELDS)),
    ]
    stator, rotor = pl.pallas_call(
        functools.partial(kernel, planes, sections),
        out_shape=(out, out),
        in_specs=[pl.BlockSpec(memory_space=pltpu.SMEM), vmem, vmem] + [hbm] * 7,
        out_specs=(vmem, vmem),
        scratch_shapes=scratch,
        compiler_params=pltpu.CompilerParams(
            collective_id=0, has_side_effects=True, vmem_limit_bytes=60 * 1024 * 1024
        ),
        name="sliding_interface",
    )(
        rot_steps,
        pair_index,
        pair_weight,
        stator_adj[:, 0],
        rotor_adj[:, 0],
        stator_rhs[:, 0],
        rotor_rhs[:, 0],
        stator_dtau[0],
        rotor_dtau[0],
        roe_jac[:, :, 0],
    )
    return stator[:, None], rotor[:, None]


def solution(mesh):
    in_specs = (
        P(None, "pitch", None, "span"),
        P(None, "pitch", None, "span"),
        P(None, "pitch", None, "span"),
        P(None, "pitch", None, "span"),
        P("pitch", None, "span"),
        P("pitch", None, "span"),
        P(None, None, "pitch", None, "span"),
        P(None, "pitch", None),
        P(None, "pitch", None),
        P(),
    )
    out_specs = (P(None, "pitch", None, "span"), P(None, "pitch", None, "span"))
    return jax.shard_map(shards, mesh=mesh, in_specs=in_specs, out_specs=out_specs, check_vma=False)
```

```python
import functools

import jax
import jax.numpy as jnp
from jax import lax
from jax.experimental import pallas as pl
from jax.experimental.pallas import tpu as pltpu
from jax.sharding import PartitionSpec as P

COMP = 5
STEPS = 2
LANES = 4
span_coupling = 0.25
MESH = pl.DeviceIdType.MESH

HOME_PLANES, HOME_LANES = 0, 1
OUT_PLANES, OUT_LANES, BACK_LANES, BACK_PLANES = 2, 3, 4, 5
END_LANES, END_PLANES = 10, 11
EDGES = 12
LOCAL = 13
STAGES = 14
FIELDS = 2 * COMP + 1


def kernel(
    planes,
    sections,
    rot_ref,
    index_ref,
    weight_ref,
    stator_hbm,
    rotor_hbm,
    stator_rhs_hbm,
    rotor_rhs_hbm,
    stator_dtau_hbm,
    rotor_dtau_hbm,
    jac_hbm,
    stator_out,
    rotor_out,
    stator_ref,
    stator_rhs_ref,
    stator_dtau_ref,
    jac_ref,
    home_in,
    home_split,
    spread,
    state,
    rolled,
    base,
    relay,
    packed,
    pair_in,
    interp,
    flux,
    credit_out,
    credit_in,
    sums,
    sums_in,
    summed,
    end_split,
    end_in,
    end_rows,
    edge_out,
    edge_in,
    weights,
    weights_t,
    send_sem,
    recv_sem,
):
    faces, span = stator_ref.shape[1:]
    strips = planes * LANES
    quarter = faces // LANES
    halves = planes // 2
    rows = faces // planes

    me = lax.axis_index("pitch")
    section = lax.axis_index("span")
    plane, lane = me // LANES, lax.rem(me, LANES)
    other_planes = [lax.rem(plane + d, planes) for d in range(1, planes)]
    other_lanes = [lax.rem(lane + d, LANES) for d in range(1, LANES)]
    left, right = lax.rem(section + sections - 1, sections), lax.rem(section + 1, sections)

    def eight(i):
        return pl.ds(pl.multiple_of(8 * i, 8), 8)

    def copy_to(src, dst, stage, n, target):
        pltpu.make_async_remote_copy(
            src, dst, send_sem.at[stage, n], recv_sem.at[stage, n], device_id=target, device_id_type=MESH
        ).start()

    def to_planes(src, dst, stage, n):
        for p in other_planes:
            copy_to(src(p), dst, stage, n, {"pitch": p * LANES + lane})

    def to_lanes(src, dst, stage, n):
        for y in other_lanes:
            copy_to(src(y), dst, stage, n, {"pitch": plane * LANES + y})

    finish = []

    def wait(buf, stage, n):
        pltpu.make_async_copy(buf, buf, recv_sem.at[stage, n]).wait()

    def arrived(buf, stage, n):
        wait(buf, stage, n)
        finish.append((buf, stage, n))

    def keep(src, dst, stage, n):
        pltpu.make_async_copy(src, dst, recv_sem.at[stage, n]).start()

    own = (
        (stator_hbm, stator_ref),
        (stator_dtau_hbm, stator_dtau_ref),
        (stator_rhs_hbm, stator_rhs_ref),
        (jac_hbm, jac_ref),
    )
    for n, (src, dst) in enumerate(own):
        keep(src, dst, LOCAL, n)

    def own_here(n):
        wait(own[n][1], LOCAL, n)

    barrier = pltpu.get_barrier_semaphore()
    for p in other_planes:
        pl.semaphore_signal(barrier, inc=1, device_id={"pitch": p * LANES + lane}, device_id_type=MESH)
    for y in other_lanes:
        pl.semaphore_signal(barrier, inc=1, device_id={"pitch": plane * LANES + y}, device_id_type=MESH)
    for t in (left, right):
        pl.semaphore_signal(barrier, inc=1, device_id={"span": t}, device_id_type=MESH)
    pl.semaphore_wait(barrier, planes - 1 + LANES - 1 + 2)

    def field(n):
        if n < COMP:
            return rotor_hbm.at[n]
        if n < 2 * COMP:
            return rotor_rhs_hbm.at[n - COMP]
        return rotor_dtau_hbm

    def send_home(n):
        src = field(n)

        def part(p):
            return src.at[pl.ds(pl.multiple_of(p * rows, rows), rows)]

        to_planes(part, home_in.at[n, plane], HOME_PLANES, n)
        keep(part(plane), home_in.at[n, plane], HOME_PLANES, n)

    def split_home(n):
        wait(home_in.at[n], HOME_PLANES, n)
        finish.append((home_in.at[n, pl.ds(0, planes - 1)], HOME_PLANES, n))

        def body(i, carry):
            one, two = home_in[n, 2 * i], home_in[n, 2 * i + 1]
            for y in range(LANES):
                home_split[n, y, eight(i)] = jnp.concatenate([one[4 * y : 4 * y + 4], two[4 * y : 4 * y + 4]], axis=0)
            return carry

        lax.fori_loop(0, halves, body, 0)
        to_lanes(lambda y: home_split.at[n, y], spread.at[n, lane], HOME_LANES, n)
        spread[n, lane] = home_split[n, lane]

    def spread_here(n):
        arrived(spread.at[n, pl.ds(0, LANES - 1)], HOME_LANES, n)

    def send_strips(step, c):
        rotation = rot_ref[step]
        places = []
        for b in range(LANES):
            offset = (b - 1 - rotation + 2 * strips) & (strips - 1)
            places.append((offset & (LANES - 1), offset >> 2))

        def body(a, carry):
            for b, (y, q) in enumerate(places):
                rolled[step, c, LANES * a + b] = state[step, c, y, (a + q) & (planes - 1)]
            return carry

        lax.fori_loop(0, planes, body, 0)
        rolled[step, c, strips] = state[step, c, places[0][0], places[0][1]]

        def part(p):
            return rolled.at[step, c, pl.ds(p * LANES, LANES + 1)]

        to_planes(part, relay.at[step, c, plane], OUT_PLANES + 4 * step, c)
        relay[step, c, plane] = rolled[step, c, pl.ds(plane * LANES, LANES + 1)]

    def first_state(c):
        def body(i, carry):
            for y in range(LANES):
                held = spread[c, y, eight(i)]
                state[0, c, y, 2 * i] = held[:4]
                state[0, c, y, 2 * i + 1] = held[4:]
            return carry

        lax.fori_loop(0, halves, body, 0)

    def pack(step, c):
        arrived(relay.at[step, c, pl.ds(0, planes - 1)], OUT_PLANES + 4 * step, c)

        def body(i, carry):
            for u in range(LANES + 1):
                packed[step, c, u, eight(i)] = jnp.concatenate(
                    [relay[step, c, 2 * i, u], relay[step, c, 2 * i + 1, u]], axis=0
                )
            return carry

        lax.fori_loop(0, halves, body, 0)
        to_lanes(
            lambda y: packed.at[step, c, pl.ds(y, 2)], pair_in.at[step, c, lane], OUT_LANES + 4 * step, c
        )
        pair_in[step, c, lane] = packed[step, c, pl.ds(lane, 2)]

    def split(x):
        high = x.astype(jnp.bfloat16)
        return high, (x - high.astype(jnp.float32)).astype(jnp.bfloat16)

    def product(table, x):
        high, low = split(x)
        total = jnp.dot(table[0], high, preferred_element_type=jnp.float32)
        total += jnp.dot(table[1], high, preferred_element_type=jnp.float32)
        return total + jnp.dot(table[0], low, preferred_element_type=jnp.float32)

    def build_weights():
        place = lax.broadcasted_iota(jnp.int32, (2 * faces, faces), 0)
        half, inner = place // faces, lax.rem(place, faces)
        y, inner = inner // quarter, lax.rem(inner, quarter)
        face = half * faces + (inner // 4) * rows + 4 * y + lax.rem(inner, 4)
        table = jnp.zeros((2 * faces, faces), jnp.float32)
        for p in range(2):
            table += jnp.where(index_ref[p] == face, weight_ref[p], 0.0)
        weights_t[0], weights_t[1] = split(table)
        weights[0], weights[1] = split(table.T)

    def interpolate(step, c):
        arrived(pair_in.at[step, c, pl.ds(0, LANES - 1)], OUT_LANES + 4 * step, c)
        paired = jnp.concatenate([pair_in[step, c, y, h] for h in range(2) for y in range(LANES)], axis=0)
        value = product(weights, paired)
        interp[c] = value
        if c < COMP - 1:
            for b in range(COMP):
                term = jac_ref[c, b].astype(jnp.float32) * value
                flux[b] = flux[b] + term if c else term

    def flux_and_credit(step, b):
        total = flux[b] + jac_ref[COMP - 1, b].astype(jnp.float32) * interp[COMP - 1]
        flux[b] = total
        credit = product(weights_t, total)
        for h in range(2):
            for y in range(LANES):
                start = h * faces + y * quarter
                credit_out[step, b, y, h] = credit[start : start + quarter]
        to_lanes(
            lambda y: credit_out.at[step, b, y], credit_in.at[step, b, lane], BACK_LANES + 4 * step, b
        )
        credit_in[step, b, lane] = credit_out[step, b, lane]

    def sum_credit(step, b):
        arrived(credit_in.at[step, b, pl.ds(0, LANES - 1)], BACK_LANES + 4 * step, b)

        def body(i, carry):
            for u in range(LANES + 1):
                if u == 0:
                    total = credit_in[step, b, 0, 0, eight(i)]
                elif u == LANES:
                    total = credit_in[step, b, LANES - 1, 1, eight(i)]
                else:
                    total = credit_in[step, b, u, 0, eight(i)] + credit_in[step, b, u - 1, 1, eight(i)]
                sums[step, b, 2 * i, u] = total[:4]
                sums[step, b, 2 * i + 1, u] = total[4:]
            return carry

        lax.fori_loop(0, halves, body, 0)
        to_planes(lambda p: sums.at[step, b, p], sums_in.at[step, b, plane], BACK_PLANES + 4 * step, b)
        sums_in[step, b, plane] = sums[step, b, plane]

    def update(step, b):
        rotation = rot_ref[step]
        arrived(sums_in.at[step, b, pl.ds(0, planes - 1)], BACK_PLANES + 4 * step, b)

        def gather(p, carry):
            for v in range(LANES - 1):
                summed[v, p] = sums_in[step, b, p, v + 1]
            after = (p + 1) & (planes - 1)
            summed[LANES - 1, p] = sums_in[step, b, p, LANES] + sums_in[step, b, after, 0]
            return carry

        lax.fori_loop(0, planes, gather, 0)
        places = []
        for y in range(LANES):
            offset = (y + rotation) & (strips - 1)
            places.append((offset & (LANES - 1), offset >> 2))

        def body(i, carry):
            for y, (v, q) in enumerate(places):
                first, second = (q + 2 * i) & (planes - 1), (q + 2 * i + 1) & (planes - 1)
                returned = jnp.concatenate([summed[v, first], summed[v, second]], axis=0)
                new = base[step, b, y, eight(i)] + spread[2 * COMP, y, eight(i)] * returned
                if step == 0:
                    state[1, b, y, 2 * i] = new[:4]
                    state[1, b, y, 2 * i + 1] = new[4:]
                    spread[b, y, eight(i)] = new
                else:
                    end_split[b, y, eight(i)] = new
            return carry

        lax.fori_loop(0, halves, body, 0)

    def send_edges(n, fetch):
        row = lax.broadcasted_iota(jnp.int32, (8, span), 0)
        col = lax.broadcasted_iota(jnp.int32, (8, span), 1)
        pick = ((row == 0) & (col == 0)) | ((row == 1) & (col == span - 1))
        pick = jnp.where(pick, 1.0, 0.0).astype(jnp.float32)
        for c in range(COMP):
            edge_out[n, c] = lax.dot_general(
                pick, fetch(c), (((1,), (1,)), ((), ())),
                precision=lax.Precision.HIGHEST, preferred_element_type=jnp.float32,
            )
        copy_to(edge_out.at[n], edge_in.at[n, 0], EDGES, 2 * n, {"span": right})
        copy_to(edge_out.at[n], edge_in.at[n, 1], EDGES, 2 * n + 1, {"span": left})

    def edges_here(n):
        arrived(edge_in.at[n, 0], EDGES, 2 * n)
        arrived(edge_in.at[n, 1], EDGES, 2 * n + 1)

    def laplace(n, c, x):
        row = lax.broadcasted_iota(jnp.int32, (16, span), 0)
        col = lax.broadcasted_iota(jnp.int32, (16, span), 1)
        place = ((row == 1) & (col == 0) & (section > 0)) | (
            (row == 8) & (col == span - 1) & (section < sections - 1)
        )
        place = jnp.where(place, 1.0, 0.0).astype(jnp.float32)
        held = jnp.concatenate([edge_in[n, 0, c], edge_in[n, 1, c]], axis=0)
        beyond = lax.dot_general(
            held, place, (((0,), (0,)), ((), ())),
            precision=lax.Precision.HIGHEST, preferred_element_type=jnp.float32,
        )
        at = lax.broadcasted_iota(jnp.int32, x.shape, 1)
        before = jnp.where(at == 0, 0.0, pltpu.roll(x, 1, 1))
        after = jnp.where(at == span - 1, 0.0, pltpu.roll(x, span - 1, 1))
        return before + after + beyond - 2.0 * x

    def spread_field(n):
        return spread[n].reshape(faces, span)

    def build_base(step, c):
        x = spread_field(c)
        change = spread_field(COMP + c) - x + span_coupling * laplace(1 + step, c, x)
        base[step, c] = (x + spread_field(2 * COMP) * change).reshape(LANES, quarter, span)

    def stator_step(step, c):
        source = stator_ref if step == 0 else stator_out
        x = source[c]
        change = stator_rhs_ref[c] - x + span_coupling * laplace(3 * step, c, x) - flux[c]
        stator_out[c] = x + stator_dtau_ref[...] * change

    def send_end(c):
        to_lanes(lambda y: end_split.at[c, y], end_in.at[c, lane], END_LANES, c)
        end_in[c, lane] = end_split[c, lane]

    def join_end(c):
        arrived(end_in.at[c, pl.ds(0, LANES - 1)], END_LANES, c)

        def body(i, carry):
            held = [end_in[c, y, eight(i)] for y in range(LANES)]
            end_rows[c, 2 * i] = jnp.concatenate([h[:4] for h in held], axis=0)
            end_rows[c, 2 * i + 1] = jnp.concatenate([h[4:] for h in held], axis=0)
            return carry

        lax.fori_loop(0, halves, body, 0)
        mine = pl.ds(pl.multiple_of(plane * rows, rows), rows)
        to_planes(lambda p: end_rows.at[c, p], rotor_out.at[c, mine], END_PLANES, c)
        keep(end_rows.at[c, plane], rotor_out.at[c, mine], END_PLANES, c)

    every = range(COMP)
    late = [2 * COMP] + [COMP + c for c in every]

    def take(c):
        spread_here(c)
        first_state(c)
        send_strips(0, c)

    def to_stator(step):
        for c in every:
            pack(step, c)
            if c:
                interpolate(step, c - 1)
            if c == COMP - 1 and step == 0:
                for n in late:
                    send_home(n)
        interpolate(step, COMP - 1)

    def to_spread(step):
        for b in every:
            flux_and_credit(step, b)
            if b >= 2:
                sum_credit(step, b - 2)
        sum_credit(step, COMP - 2)
        sum_credit(step, COMP - 1)

    for c in every:
        send_home(c)
    own_here(0)
    send_edges(0, lambda c: stator_ref[c])
    build_weights()
    for c in every:
        split_home(c)
        if c:
            take(c - 1)
    take(COMP - 1)
    send_edges(1, spread_field)
    own_here(3)
    to_stator(0)
    to_spread(0)
    edges_here(0)
    own_here(1)
    own_here(2)
    for n in late[:2]:
        split_home(n)
    for c in every:
        stator_step(0, c)
    send_edges(3, lambda c: stator_out[c])
    edges_here(1)
    spread_here(2 * COMP)
    for b in every:
        if b < COMP - 1:
            split_home(late[b + 2])
        spread_here(COMP + b)
        build_base(0, b)
        update(0, b)
        send_strips(1, b)
    send_edges(2, spread_field)
    to_stator(1)
    to_spread(1)
    edges_here(2)
    for c in every:
        build_base(1, c)
    edges_here(3)
    for b in every:
        update(1, b)
        send_end(b)
        if b:
            join_end(b - 1)
    join_end(COMP - 1)
    for c in every:
        stator_step(1, c)
    for c in every:
        wait(rotor_out.at[c], END_PLANES, c)
        finish.append((rotor_out.at[c, pl.ds(0, (planes - 1) * rows)], END_PLANES, c))
    for buf, stage, n in finish:
        pltpu.make_async_copy(buf, buf, send_sem.at[stage, n]).wait()


def shards(
    stator_adj,
    rotor_adj,
    stator_rhs,
    rotor_rhs,
    stator_dtau,
    rotor_dtau,
    roe_jac,
    pair_index,
    pair_weight,
    rot_steps,
):
    _, _, faces, span = stator_adj.shape
    planes = lax.axis_size("pitch") // LANES
    sections = lax.axis_size("span")
    quarter, rows = faces // LANES, faces // planes
    f32, bf16 = jnp.float32, jnp.bfloat16
    vmem = pl.BlockSpec(memory_space=pltpu.VMEM)
    hbm = pl.BlockSpec(memory_space=pl.ANY)
    out = pltpu.VMEM((COMP, faces, span), f32)
    strips = planes * LANES
    scratch = [
        pltpu.VMEM((COMP, faces, span), f32),
        pltpu.VMEM((COMP, faces, span), f32),
        pltpu.VMEM((faces, span), f32),
        pltpu.VMEM((COMP, COMP, faces, span), bf16),
        pltpu.VMEM((FIELDS, planes, rows, span), f32),
        pltpu.VMEM((FIELDS, LANES, quarter, span), f32),
        pltpu.VMEM((FIELDS, LANES, quarter, span), f32),
        pltpu.VMEM((STEPS, COMP, LANES, planes, 4, span), f32),
        pltpu.VMEM((STEPS, COMP, strips + 1, 4, span), f32),
        pltpu.VMEM((STEPS, COMP, LANES, quarter, span), f32),
        pltpu.VMEM((STEPS, COMP, planes, LANES + 1, 4, span), f32),
        pltpu.VMEM((STEPS, COMP, LANES + 1, quarter, span), f32),
        pltpu.VMEM((STEPS, COMP, LANES, 2, quarter, span), f32),
        pltpu.VMEM((COMP, faces, span), f32),
        pltpu.VMEM((COMP, faces, span), f32),
        pltpu.VMEM((STEPS, COMP, LANES, 2, quarter, span), f32),
        pltpu.VMEM((STEPS, COMP, LANES, 2, quarter, span), f32),
        pltpu.VMEM((STEPS, COMP, planes, LANES + 1, 4, span), f32),
        pltpu.VMEM((STEPS, COMP, planes, LANES + 1, 4, span), f32),
        pltpu.VMEM((LANES, planes, 4, span), f32),
        pltpu.VMEM((COMP, LANES, quarter, span), f32),
        pltpu.VMEM((COMP, LANES, quarter, span), f32),
        pltpu.VMEM((COMP, planes, rows, span), f32),
        pltpu.VMEM((4, COMP, 8, faces), f32),
        pltpu.VMEM((4, 2, COMP, 8, faces), f32),
        pltpu.VMEM((2, faces, 2 * faces), bf16),
        pltpu.VMEM((2, 2 * faces, faces), bf16),
        pltpu.SemaphoreType.DMA((STAGES, FIELDS)),
        pltpu.SemaphoreType.DMA((STAGES, FIELDS)),
    ]
    stator, rotor = pl.pallas_call(
        functools.partial(kernel, planes, sections),
        out_shape=(out, out),
        in_specs=[pl.BlockSpec(memory_space=pltpu.SMEM), vmem, vmem] + [hbm] * 7,
        out_specs=(vmem, vmem),
        scratch_shapes=scratch,
        compiler_params=pltpu.CompilerParams(
            collective_id=0, has_side_effects=True, vmem_limit_bytes=60 * 1024 * 1024
        ),
        name="sliding_interface",
    )(
        rot_steps,
        pair_index,
        pair_weight,
        stator_adj[:, 0],
        rotor_adj[:, 0],
        stator_rhs[:, 0],
        rotor_rhs[:, 0],
        stator_dtau[0],
        rotor_dtau[0],
        roe_jac[:, :, 0],
    )
    return stator[:, None], rotor[:, None]


def solution(mesh):
    in_specs = (
        P(None, "pitch", None, "span"),
        P(None, "pitch", None, "span"),
        P(None, "pitch", None, "span"),
        P(None, "pitch", None, "span"),
        P("pitch", None, "span"),
        P("pitch", None, "span"),
        P(None, None, "pitch", None, "span"),
        P(None, "pitch", None),
        P(None, "pitch", None),
        P(),
    )
    out_specs = (P(None, "pitch", None, "span"), P(None, "pitch", None, "span"))
    return jax.shard_map(shards, mesh=mesh, in_specs=in_specs, out_specs=out_specs, check_vma=False)
```

```python
import functools

import jax
import jax.numpy as jnp
from jax import lax
from jax.experimental import pallas as pl
from jax.experimental.pallas import tpu as pltpu
from jax.sharding import PartitionSpec as P

COMP = 5
STEPS = 2
LANES = 4
span_coupling = 0.25
MESH = pl.DeviceIdType.MESH

HOME_PLANES, HOME_LANES = 0, 1
OUT_PLANES, OUT_LANES, BACK_LANES, BACK_PLANES = 2, 3, 4, 5
END_LANES, END_PLANES = 10, 11
EDGES = 12
LOCAL = 13
STAGES = 14
FIELDS = 2 * COMP + 1


def kernel(
    planes,
    sections,
    rot_ref,
    index_ref,
    weight_ref,
    stator_hbm,
    rotor_hbm,
    stator_rhs_hbm,
    rotor_rhs_hbm,
    stator_dtau_hbm,
    rotor_dtau_hbm,
    jac_hbm,
    stator_out,
    rotor_out,
    stator_ref,
    stator_rhs_ref,
    stator_dtau_ref,
    jac_ref,
    home_in,
    home_split,
    spread,
    state,
    rolled,
    base,
    relay,
    packed,
    pair_in,
    interp,
    flux,
    credit_out,
    credit_in,
    sums,
    sums_in,
    summed,
    end_split,
    end_in,
    end_rows,
    edge_out,
    edge_in,
    weights,
    weights_t,
    send_sem,
    recv_sem,
):
    faces, span = stator_ref.shape[1:]
    strips = planes * LANES
    quarter = faces // LANES
    halves = planes // 2
    rows = faces // planes

    me = lax.axis_index("pitch")
    section = lax.axis_index("span")
    plane, lane = me // LANES, lax.rem(me, LANES)
    other_planes = [lax.rem(plane + d, planes) for d in range(1, planes)]
    other_lanes = [lax.rem(lane + d, LANES) for d in range(1, LANES)]
    left, right = lax.rem(section + sections - 1, sections), lax.rem(section + 1, sections)

    def eight(i):
        return pl.ds(pl.multiple_of(8 * i, 8), 8)

    def copy_to(src, dst, stage, n, target):
        pltpu.make_async_remote_copy(
            src, dst, send_sem.at[stage, n], recv_sem.at[stage, n], device_id=target, device_id_type=MESH
        ).start()

    def to_planes(src, dst, stage, n):
        for p in other_planes:
            copy_to(src(p), dst, stage, n, {"pitch": p * LANES + lane})

    def to_lanes(src, dst, stage, n):
        for y in other_lanes:
            copy_to(src(y), dst, stage, n, {"pitch": plane * LANES + y})

    finish = []

    def wait(buf, stage, n):
        pltpu.make_async_copy(buf, buf, recv_sem.at[stage, n]).wait()

    def arrived(buf, stage, n):
        wait(buf, stage, n)
        finish.append((buf, stage, n))

    def keep(src, dst, stage, n):
        pltpu.make_async_copy(src, dst, recv_sem.at[stage, n]).start()

    own = (
        (stator_hbm, stator_ref),
        (stator_dtau_hbm, stator_dtau_ref),
        (stator_rhs_hbm, stator_rhs_ref),
        (jac_hbm, jac_ref),
    )
    for n, (src, dst) in enumerate(own):
        keep(src, dst, LOCAL, n)

    def own_here(n):
        wait(own[n][1], LOCAL, n)

    barrier = pltpu.get_barrier_semaphore()
    for p in other_planes:
        pl.semaphore_signal(barrier, inc=1, device_id={"pitch": p * LANES + lane}, device_id_type=MESH)
    for y in other_lanes:
        pl.semaphore_signal(barrier, inc=1, device_id={"pitch": plane * LANES + y}, device_id_type=MESH)
    for t in (left, right):
        pl.semaphore_signal(barrier, inc=1, device_id={"span": t}, device_id_type=MESH)
    pl.semaphore_wait(barrier, planes - 1 + LANES - 1 + 2)

    def field(n):
        if n < COMP:
            return rotor_hbm.at[n]
        if n < 2 * COMP:
            return rotor_rhs_hbm.at[n - COMP]
        return rotor_dtau_hbm

    def send_home(n):
        src = field(n)

        def part(p):
            return src.at[pl.ds(pl.multiple_of(p * rows, rows), rows)]

        to_planes(part, home_in.at[n, plane], HOME_PLANES, n)
        keep(part(plane), home_in.at[n, plane], HOME_PLANES, n)

    def split_home(n):
        wait(home_in.at[n], HOME_PLANES, n)
        finish.append((home_in.at[n, pl.ds(0, planes - 1)], HOME_PLANES, n))

        def body(i, carry):
            one, two = home_in[n, 2 * i], home_in[n, 2 * i + 1]
            for y in range(LANES):
                home_split[n, y, eight(i)] = jnp.concatenate([one[4 * y : 4 * y + 4], two[4 * y : 4 * y + 4]], axis=0)
            return carry

        lax.fori_loop(0, halves, body, 0)
        to_lanes(lambda y: home_split.at[n, y], spread.at[n, lane], HOME_LANES, n)
        spread[n, lane] = home_split[n, lane]

    def spread_here(n):
        arrived(spread.at[n, pl.ds(0, LANES - 1)], HOME_LANES, n)

    def send_strips(step, c):
        rotation = rot_ref[step]
        places = []
        for b in range(LANES):
            offset = (b - 1 - rotation + 2 * strips) & (strips - 1)
            places.append((offset & (LANES - 1), offset >> 2))

        def body(a, carry):
            for b, (y, q) in enumerate(places):
                rolled[step, c, LANES * a + b] = state[step, c, y, (a + q) & (planes - 1)]
            return carry

        lax.fori_loop(0, planes, body, 0)
        rolled[step, c, strips] = state[step, c, places[0][0], places[0][1]]

        def part(p):
            return rolled.at[step, c, pl.ds(p * LANES, LANES + 1)]

        to_planes(part, relay.at[step, c, plane], OUT_PLANES + 4 * step, c)
        relay[step, c, plane] = rolled[step, c, pl.ds(plane * LANES, LANES + 1)]

    def first_state(c):
        def body(i, carry):
            for y in range(LANES):
                held = spread[c, y, eight(i)]
                state[0, c, y, 2 * i] = held[:4]
                state[0, c, y, 2 * i + 1] = held[4:]
            return carry

        lax.fori_loop(0, halves, body, 0)

    def pack(step, c):
        arrived(relay.at[step, c, pl.ds(0, planes - 1)], OUT_PLANES + 4 * step, c)

        def body(i, carry):
            for u in range(LANES + 1):
                packed[step, c, u, eight(i)] = jnp.concatenate(
                    [relay[step, c, 2 * i, u], relay[step, c, 2 * i + 1, u]], axis=0
                )
            return carry

        lax.fori_loop(0, halves, body, 0)
        to_lanes(
            lambda y: packed.at[step, c, pl.ds(y, 2)], pair_in.at[step, c, lane], OUT_LANES + 4 * step, c
        )
        pair_in[step, c, lane] = packed[step, c, pl.ds(lane, 2)]

    def split(x):
        high = x.astype(jnp.bfloat16)
        return high, (x - high.astype(jnp.float32)).astype(jnp.bfloat16)

    def product(table, x):
        high, low = split(x)
        total = jnp.dot(table[0], high, preferred_element_type=jnp.float32)
        total += jnp.dot(table[1], high, preferred_element_type=jnp.float32)
        return total + jnp.dot(table[0], low, preferred_element_type=jnp.float32)

    def build_weights():
        place = lax.broadcasted_iota(jnp.int32, (2 * faces, faces), 0)
        half, inner = place // faces, lax.rem(place, faces)
        y, inner = inner // quarter, lax.rem(inner, quarter)
        face = half * faces + (inner // 4) * rows + 4 * y + lax.rem(inner, 4)
        table = jnp.zeros((2 * faces, faces), jnp.float32)
        for p in range(2):
            table += jnp.where(index_ref[p] == face, weight_ref[p], 0.0)
        weights_t[0], weights_t[1] = split(table)
        weights[0], weights[1] = split(table.T)

    def interpolate(step, c):
        arrived(pair_in.at[step, c, pl.ds(0, LANES - 1)], OUT_LANES + 4 * step, c)
        paired = jnp.concatenate([pair_in[step, c, y, h] for h in range(2) for y in range(LANES)], axis=0)
        value = product(weights, paired)
        interp[c] = value
        if c < COMP - 1:
            for b in range(COMP):
                term = jac_ref[c, b].astype(jnp.float32) * value
                flux[b] = flux[b] + term if c else term

    def flux_and_credit(step, b):
        total = flux[b] + jac_ref[COMP - 1, b].astype(jnp.float32) * interp[COMP - 1]
        flux[b] = total
        credit = product(weights_t, total)
        for h in range(2):
            for y in range(LANES):
                start = h * faces + y * quarter
                credit_out[step, b, y, h] = credit[start : start + quarter]
        to_lanes(
            lambda y: credit_out.at[step, b, y], credit_in.at[step, b, lane], BACK_LANES + 4 * step, b
        )
        credit_in[step, b, lane] = credit_out[step, b, lane]

    def sum_credit(step, b):
        arrived(credit_in.at[step, b, pl.ds(0, LANES - 1)], BACK_LANES + 4 * step, b)

        def body(i, carry):
            for u in range(LANES + 1):
                if u == 0:
                    total = credit_in[step, b, 0, 0, eight(i)]
                elif u == LANES:
                    total = credit_in[step, b, LANES - 1, 1, eight(i)]
                else:
                    total = credit_in[step, b, u, 0, eight(i)] + credit_in[step, b, u - 1, 1, eight(i)]
                sums[step, b, 2 * i, u] = total[:4]
                sums[step, b, 2 * i + 1, u] = total[4:]
            return carry

        lax.fori_loop(0, halves, body, 0)
        to_planes(lambda p: sums.at[step, b, p], sums_in.at[step, b, plane], BACK_PLANES + 4 * step, b)
        sums_in[step, b, plane] = sums[step, b, plane]

    def update(step, b):
        rotation = rot_ref[step]
        arrived(sums_in.at[step, b, pl.ds(0, planes - 1)], BACK_PLANES + 4 * step, b)

        def gather(p, carry):
            for v in range(LANES - 1):
                summed[v, p] = sums_in[step, b, p, v + 1]
            after = (p + 1) & (planes - 1)
            summed[LANES - 1, p] = sums_in[step, b, p, LANES] + sums_in[step, b, after, 0]
            return carry

        lax.fori_loop(0, planes, gather, 0)
        places = []
        for y in range(LANES):
            offset = (y + rotation) & (strips - 1)
            places.append((offset & (LANES - 1), offset >> 2))

        def body(i, carry):
            for y, (v, q) in enumerate(places):
                first, second = (q + 2 * i) & (planes - 1), (q + 2 * i + 1) & (planes - 1)
                returned = jnp.concatenate([summed[v, first], summed[v, second]], axis=0)
                new = base[step, b, y, eight(i)] + spread[2 * COMP, y, eight(i)] * returned
                if step == 0:
                    state[1, b, y, 2 * i] = new[:4]
                    state[1, b, y, 2 * i + 1] = new[4:]
                    spread[b, y, eight(i)] = new
                else:
                    end_split[b, y, eight(i)] = new
            return carry

        lax.fori_loop(0, halves, body, 0)

    def send_edges(n, fetch):
        row = lax.broadcasted_iota(jnp.int32, (8, span), 0)
        col = lax.broadcasted_iota(jnp.int32, (8, span), 1)
        pick = ((row == 0) & (col == 0)) | ((row == 1) & (col == span - 1))
        pick = jnp.where(pick, 1.0, 0.0).astype(jnp.float32)
        for c in range(COMP):
            edge_out[n, c] = lax.dot_general(
                pick, fetch(c), (((1,), (1,)), ((), ())),
                precision=lax.Precision.HIGHEST, preferred_element_type=jnp.float32,
            )
        copy_to(edge_out.at[n], edge_in.at[n, 0], EDGES, 2 * n, {"span": right})
        copy_to(edge_out.at[n], edge_in.at[n, 1], EDGES, 2 * n + 1, {"span": left})

    def edges_here(n):
        arrived(edge_in.at[n, 0], EDGES, 2 * n)
        arrived(edge_in.at[n, 1], EDGES, 2 * n + 1)

    def laplace(n, c, x):
        row = lax.broadcasted_iota(jnp.int32, (16, span), 0)
        col = lax.broadcasted_iota(jnp.int32, (16, span), 1)
        place = ((row == 1) & (col == 0) & (section > 0)) | (
            (row == 8) & (col == span - 1) & (section < sections - 1)
        )
        place = jnp.where(place, 1.0, 0.0).astype(jnp.float32)
        held = jnp.concatenate([edge_in[n, 0, c], edge_in[n, 1, c]], axis=0)
        beyond = lax.dot_general(
            held, place, (((0,), (0,)), ((), ())),
            precision=lax.Precision.HIGHEST, preferred_element_type=jnp.float32,
        )
        at = lax.broadcasted_iota(jnp.int32, x.shape, 1)
        before = jnp.where(at == 0, 0.0, pltpu.roll(x, 1, 1))
        after = jnp.where(at == span - 1, 0.0, pltpu.roll(x, span - 1, 1))
        return before + after + beyond - 2.0 * x

    def spread_field(n):
        return spread[n].reshape(faces, span)

    def build_base(step, c):
        x = spread_field(c)
        change = spread_field(COMP + c) - x + span_coupling * laplace(1 + step, c, x)
        base[step, c] = (x + spread_field(2 * COMP) * change).reshape(LANES, quarter, span)

    def stator_step(step, c):
        source = stator_ref if step == 0 else stator_out
        x = source[c]
        change = stator_rhs_ref[c] - x + span_coupling * laplace(3 * step, c, x) - flux[c]
        stator_out[c] = x + stator_dtau_ref[...] * change

    def send_end(c):
        to_lanes(lambda y: end_split.at[c, y], end_in.at[c, lane], END_LANES, c)
        end_in[c, lane] = end_split[c, lane]

    def join_end(c):
        arrived(end_in.at[c, pl.ds(0, LANES - 1)], END_LANES, c)

        def body(i, carry):
            held = [end_in[c, y, eight(i)] for y in range(LANES)]
            end_rows[c, 2 * i] = jnp.concatenate([h[:4] for h in held], axis=0)
            end_rows[c, 2 * i + 1] = jnp.concatenate([h[4:] for h in held], axis=0)
            return carry

        lax.fori_loop(0, halves, body, 0)
        mine = pl.ds(pl.multiple_of(plane * rows, rows), rows)
        to_planes(lambda p: end_rows.at[c, p], rotor_out.at[c, mine], END_PLANES, c)
        keep(end_rows.at[c, plane], rotor_out.at[c, mine], END_PLANES, c)

    every = range(COMP)
    late = [2 * COMP] + [COMP + c for c in every]

    def take(c):
        spread_here(c)
        first_state(c)
        send_strips(0, c)

    def to_stator(step):
        for c in every:
            pack(step, c)
            if c == (COMP - 1 if step else 2):
                send_edges(1 + step, spread_field)
            if c:
                interpolate(step, c - 1)
            if c == COMP - 1 and step == 0:
                for n in late:
                    send_home(n)
        interpolate(step, COMP - 1)

    def to_spread(step):
        for b in every:
            flux_and_credit(step, b)
            if b >= 2:
                sum_credit(step, b - 2)
        sum_credit(step, COMP - 2)
        sum_credit(step, COMP - 1)

    for c in every:
        send_home(c)
    own_here(0)
    send_edges(0, lambda c: stator_ref[c])
    build_weights()
    for c in every:
        split_home(c)
        if c:
            take(c - 1)
    take(COMP - 1)
    own_here(3)
    to_stator(0)
    to_spread(0)
    edges_here(0)
    own_here(1)
    own_here(2)
    for n in late[:2]:
        split_home(n)
    for c in every:
        stator_step(0, c)
    send_edges(3, lambda c: stator_out[c])
    edges_here(1)
    spread_here(2 * COMP)
    for b in every:
        if b < COMP - 1:
            split_home(late[b + 2])
        spread_here(COMP + b)
        build_base(0, b)
        update(0, b)
        send_strips(1, b)
    to_stator(1)
    to_spread(1)
    edges_here(2)
    for c in every:
        build_base(1, c)
    edges_here(3)
    for b in every:
        update(1, b)
        send_end(b)
        if b:
            join_end(b - 1)
    join_end(COMP - 1)
    for c in every:
        stator_step(1, c)
    for c in every:
        wait(rotor_out.at[c], END_PLANES, c)
        finish.append((rotor_out.at[c, pl.ds(0, (planes - 1) * rows)], END_PLANES, c))
    for buf, stage, n in finish:
        pltpu.make_async_copy(buf, buf, send_sem.at[stage, n]).wait()


def shards(
    stator_adj,
    rotor_adj,
    stator_rhs,
    rotor_rhs,
    stator_dtau,
    rotor_dtau,
    roe_jac,
    pair_index,
    pair_weight,
    rot_steps,
):
    _, _, faces, span = stator_adj.shape
    planes = lax.axis_size("pitch") // LANES
    sections = lax.axis_size("span")
    quarter, rows = faces // LANES, faces // planes
    f32, bf16 = jnp.float32, jnp.bfloat16
    vmem = pl.BlockSpec(memory_space=pltpu.VMEM)
    hbm = pl.BlockSpec(memory_space=pl.ANY)
    out = pltpu.VMEM((COMP, faces, span), f32)
    strips = planes * LANES
    scratch = [
        pltpu.VMEM((COMP, faces, span), f32),
        pltpu.VMEM((COMP, faces, span), f32),
        pltpu.VMEM((faces, span), f32),
        pltpu.VMEM((COMP, COMP, faces, span), bf16),
        pltpu.VMEM((FIELDS, planes, rows, span), f32),
        pltpu.VMEM((FIELDS, LANES, quarter, span), f32),
        pltpu.VMEM((FIELDS, LANES, quarter, span), f32),
        pltpu.VMEM((STEPS, COMP, LANES, planes, 4, span), f32),
        pltpu.VMEM((STEPS, COMP, strips + 1, 4, span), f32),
        pltpu.VMEM((STEPS, COMP, LANES, quarter, span), f32),
        pltpu.VMEM((STEPS, COMP, planes, LANES + 1, 4, span), f32),
        pltpu.VMEM((STEPS, COMP, LANES + 1, quarter, span), f32),
        pltpu.VMEM((STEPS, COMP, LANES, 2, quarter, span), f32),
        pltpu.VMEM((COMP, faces, span), f32),
        pltpu.VMEM((COMP, faces, span), f32),
        pltpu.VMEM((STEPS, COMP, LANES, 2, quarter, span), f32),
        pltpu.VMEM((STEPS, COMP, LANES, 2, quarter, span), f32),
        pltpu.VMEM((STEPS, COMP, planes, LANES + 1, 4, span), f32),
        pltpu.VMEM((STEPS, COMP, planes, LANES + 1, 4, span), f32),
        pltpu.VMEM((LANES, planes, 4, span), f32),
        pltpu.VMEM((COMP, LANES, quarter, span), f32),
        pltpu.VMEM((COMP, LANES, quarter, span), f32),
        pltpu.VMEM((COMP, planes, rows, span), f32),
        pltpu.VMEM((4, COMP, 8, faces), f32),
        pltpu.VMEM((4, 2, COMP, 8, faces), f32),
        pltpu.VMEM((2, faces, 2 * faces), bf16),
        pltpu.VMEM((2, 2 * faces, faces), bf16),
        pltpu.SemaphoreType.DMA((STAGES, FIELDS)),
        pltpu.SemaphoreType.DMA((STAGES, FIELDS)),
    ]
    stator, rotor = pl.pallas_call(
        functools.partial(kernel, planes, sections),
        out_shape=(out, out),
        in_specs=[pl.BlockSpec(memory_space=pltpu.SMEM), vmem, vmem] + [hbm] * 7,
        out_specs=(vmem, vmem),
        scratch_shapes=scratch,
        compiler_params=pltpu.CompilerParams(
            collective_id=0, has_side_effects=True, vmem_limit_bytes=60 * 1024 * 1024
        ),
        name="sliding_interface",
    )(
        rot_steps,
        pair_index,
        pair_weight,
        stator_adj[:, 0],
        rotor_adj[:, 0],
        stator_rhs[:, 0],
        rotor_rhs[:, 0],
        stator_dtau[0],
        rotor_dtau[0],
        roe_jac[:, :, 0],
    )
    return stator[:, None], rotor[:, None]


def solution(mesh):
    in_specs = (
        P(None, "pitch", None, "span"),
        P(None, "pitch", None, "span"),
        P(None, "pitch", None, "span"),
        P(None, "pitch", None, "span"),
        P("pitch", None, "span"),
        P("pitch", None, "span"),
        P(None, None, "pitch", None, "span"),
        P(None, "pitch", None),
        P(None, "pitch", None),
        P(),
    )
    out_specs = (P(None, "pitch", None, "span"), P(None, "pitch", None, "span"))
    return jax.shard_map(shards, mesh=mesh, in_specs=in_specs, out_specs=out_specs, check_vma=False)
```
